32 devices in a mesh: groups: 2 (over x), shard: 16 (over z, y, core).
Axes of the slice: x: 2, y: 2, z: 4, core: 2. Of those that a mesh axis runs over, the one named last changes fastest.
Arguments:
- residual_in: bfloat16 [128, 5120], P('groups', 'shard'), parts along dimension 0, may hold values from -12 to 12
- queries: bfloat16 [64, 16, 640], P(('groups', 'shard')), parts along dimension 0, may hold values from -8 to 8
- key_cache: bfloat16 [64, 4096, 128], P(('groups', 'shard')), parts along dimension 0, may hold values from -6 to 6
- value_cache: bfloat16 [64, 4096, 128], P(('groups', 'shard')), parts along dimension 0, may hold values from -6 to 6
- new_keys: bfloat16 [64, 16, 128], P(('groups', 'shard')), parts along dimension 0, may hold values from -8 to 8
- new_values: bfloat16 [64, 16, 128], P(('groups', 'shard')), parts along dimension 0, may hold values from -6 to 6
- cache_len: int32 [8], P('groups'), parts along dimension 0, may hold values from 1024 to 4096, as said below
- tree_mask: int32 [8, 16, 16], P('groups'), parts along dimension 0, may hold values from 0 to 1, as said below
- out_proj: bfloat16 [5120, 5120], P(None, 'shard'), may hold values from -0.25 to 0.25
- norm_gain: bfloat16 [5120], P('shard'), may hold values from 0.099609375 to 1.8984375
- gate_w: bfloat16 [5120, 27648], P(None, 'shard'), may hold values from -0.078125 to 0.078125
- up_w: bfloat16 [5120, 27648], P(None, 'shard'), may hold values from -0.078125 to 0.078125
- down_w: bfloat16 [27648, 5120], P('shard'), may hold values from -0.0390625 to 0.0390625
Outputs:
- layer_out: bfloat16 [128, 5120], P(('groups', 'shard')), parts along dimension 0
The draws below stay inside these ranges and needn't reach their ends.
There are 2 independent parts, one for each index of `groups`. The reference program is written for one: setup_inputs(seed, part) draws one part's arguments, and reference() takes and returns one part's arrays. A program takes and returns all parts, laid end to end along the dimension named above; an argument that names none is the same for every part. Nothing has to cross between parts.
Inputs may be any that keep to these rules, and one draw needn't show every extreme that they name: Positions 0 to cache_len[r] - 1 of request r's blocks are valid; some request fills all 4096 positions. tree_mask[r, i, j] is 1 exactly where draft row j is row i itself or an ancestor of row i in request r's draft tree; a row's parent comes before it, and row 0 is the root.
All inputs are finite; a program needn't handle non-finite values.
Results may differ from the reference program's by a relative error of at most 0.0059.
Values may be sent and summed in bfloat16 or wider, within the bound.
A program may use at most 128 MiB of HBM per device.

```python
import math
import jax
import jax.numpy as jnp
from jax import lax

D = 5120
FF = 27648
HQ = 40
KV = 8
HD = 128
L = 4096
DR = 16
G = 5
PAIRS = 32
REQ = 4
ROWS = 64


def draw_residual_in(key, part):
    column_pos = jnp.arange(D, dtype=jnp.float32) / D
    jitter = jax.random.uniform(jax.random.fold_in(key, 11), (D,), jnp.float32, 0.7, 1.4)
    column_scale = 0.5 * jnp.power(3.0, column_pos) * jitter
    values = jax.random.normal(jax.random.fold_in(key, 12), (ROWS, D), jnp.float32) * column_scale[None, :]
    return jnp.clip(values, -12.0, 12.0).astype(jnp.bfloat16)


def draw_queries(key, part):
    values = jnp.clip(2.0 * jax.random.normal(jax.random.fold_in(key, 21), (PAIRS, DR, G * HD), jnp.float32), -8.0, 8.0)
    return values.astype(jnp.bfloat16)


def draw_key_cache(key, part):
    values = jnp.clip(jax.random.normal(jax.random.fold_in(key, 22), (PAIRS, L, HD), jnp.float32), -6.0, 6.0)
    return values.astype(jnp.bfloat16)


def draw_cache_len(key, part):
    lengths = jax.random.randint(jax.random.fold_in(key, 31), (REQ,), L // 4, L + 1)
    selected_entry = jax.random.randint(jax.random.fold_in(key, 32), (), 0, REQ)
    return jnp.where(jnp.arange(REQ, dtype=jnp.int32) == selected_entry, L, lengths).astype(jnp.int32)


def draw_tree_mask(key, part):
    positions = jnp.arange(DR, dtype=jnp.int32)
    parent = jax.random.randint(jax.random.fold_in(key, 41), (REQ, DR), 0, jnp.maximum(positions, 1)[None, :])
    parent_link = ((parent[:, :, None] == positions[None, None, :]) & (positions[None, :, None] > 0)).astype(jnp.int32)
    identity = jnp.broadcast_to(jnp.eye(DR, dtype=jnp.int32), (REQ, DR, DR))
    reached = identity
    current = identity
    for repeat_factor in range(DR):
        current = jnp.minimum(jnp.einsum('rij,rjk->rik', current, parent_link), 1)
        reached = jnp.maximum(reached, current)
    return reached.astype(jnp.int32)


def level_of(rng, dims, split, low, high):
    factor_of, own = 1.0, jax.random.fold_in(rng, 6)
    for dim, shards_of in split:
        draws = jnp.exp(jax.random.uniform(jax.random.fold_in(own, dim), (shards_of,), jnp.float32, low / len(split), high / len(split)))
        factor_of = factor_of * jnp.repeat(draws, dims[dim] // shards_of).reshape([-1 if axis == dim else 1 for axis in range(len(dims))])
    return factor_of


def centred(key, shape, deviation, most, shards=(), kind=jnp.bfloat16):
    factor_of = level_of(key, shape, shards, -0.22, 0.18) if shards else 1.0
    values = jax.random.normal(key, shape, jnp.float32) * deviation * factor_of
    return jnp.minimum(jnp.maximum(values, -most), most).astype(kind)


def setup_inputs(seed: int = 0, part: int = 0) -> dict:
    keys = jax.random.split(jax.random.key(seed), 14)
    part_splits = jax.random.split(jax.random.fold_in(keys[13], part), 14)
    residual_in = draw_residual_in(jax.random.fold_in(jax.random.fold_in(keys[13], part), 71), part)
    queries = draw_queries(jax.random.fold_in(jax.random.fold_in(keys[13], part), 71), part)
    key_cache = draw_key_cache(jax.random.fold_in(jax.random.fold_in(keys[13], part), 71), part)
    value_cache = centred(part_splits[3], (PAIRS, L, HD), 1.0, 6.0, ((0, 16),))
    new_keys = centred(part_splits[4], (PAIRS, DR, HD), 2.0, 8.0, ((0, 16),))
    new_values = centred(part_splits[5], (PAIRS, DR, HD), 1.0, 6.0, ((0, 16),))
    cache_len = draw_cache_len(jax.random.fold_in(jax.random.fold_in(keys[13], part), 71), part)
    tree_mask = draw_tree_mask(jax.random.fold_in(jax.random.fold_in(keys[13], part), 71), part)
    out_proj = centred(keys[8], (HQ * HD, D), (G * HD) ** -0.5, 0.25, ((1, 16),))
    norm_gain = jnp.clip(1.0 + 0.18 * jax.random.normal(keys[9], (D,), jnp.float32), 0.099609375, 1.8984375).astype(jnp.bfloat16)
    gate_w = centred(keys[10], (D, FF), D ** -0.5, 0.078125, ((1, 16),))
    up_w = centred(keys[11], (D, FF), D ** -0.5, 0.078125, ((1, 16),))
    down_w = centred(keys[12], (FF, D), FF ** -0.5, 0.0390625, ((0, 16),))
    return {"residual_in": residual_in, "queries": queries, "key_cache": key_cache, "value_cache": value_cache, "new_keys": new_keys, "new_values": new_values, "cache_len": cache_len, "tree_mask": tree_mask, "out_proj": out_proj, "norm_gain": norm_gain, "gate_w": gate_w, "up_w": up_w, "down_w": down_w}


def attend_pair(query_matrix, cache_keys, cache_values, draft_keys, draft_values, length, tree):
    head_rows = query_matrix.astype(jnp.float32).reshape(DR, G, HD)
    score_scale = 1.0 / math.sqrt(HD)
    cache_scores = jnp.einsum('dgk,lk->dgl', head_rows, cache_keys.astype(jnp.float32)) * score_scale
    draft_scores = jnp.einsum('dgk,ek->dge', head_rows, draft_keys.astype(jnp.float32)) * score_scale
    valid_keys = jnp.arange(L, dtype=jnp.int32) < length
    cache_scores = jnp.where(valid_keys[None, None, :], cache_scores, -1e+30)
    draft_scores = jnp.where(tree[:, None, :] > 0, draft_scores, -1e+30)
    peak_score = jnp.maximum(lax.optimization_barrier(jnp.max(cache_scores, axis=-1)), lax.optimization_barrier(jnp.max(draft_scores, axis=-1)))
    cache_weights = jnp.where(valid_keys[None, None, :], jnp.exp(cache_scores - peak_score[..., None]), 0.0)
    draft_weights = jnp.where(tree[:, None, :] > 0, jnp.exp(draft_scores - peak_score[..., None]), 0.0)
    denom = lax.optimization_barrier(jnp.sum(cache_weights, axis=-1)) + lax.optimization_barrier(jnp.sum(draft_weights, axis=-1))
    cache_low = cache_weights.astype(jnp.bfloat16).astype(jnp.float32)
    draft_low = draft_weights.astype(jnp.bfloat16).astype(jnp.float32)
    weighted = jnp.einsum('dgl,lk->dgk', cache_low, cache_values.astype(jnp.float32))
    weighted = weighted + jnp.einsum('dge,ek->dgk', draft_low, draft_values.astype(jnp.float32))
    return (weighted / denom[..., None]).astype(jnp.bfloat16).reshape(DR, G * HD)

def reference(residual_in, queries, key_cache, value_cache, new_keys, new_values, cache_len, tree_mask, out_proj, norm_gain, gate_w, up_w, down_w):

    def one_pair(pair):
        request = pair % REQ
        return attend_pair(queries[pair], key_cache[pair], value_cache[pair], new_keys[pair], new_values[pair], cache_len[request], tree_mask[request])
    attn = lax.map(one_pair, jnp.arange(PAIRS, dtype=jnp.int32))
    grouped = attn.astype(jnp.float32).reshape(KV, REQ, DR, G * HD)
    head_projection = out_proj.astype(jnp.float32).reshape(KV, G * HD, D)
    mixed = jnp.einsum('hrdf,hfc->rdc', grouped, head_projection).reshape(ROWS, D)
    stream = (residual_in.astype(jnp.float32) + mixed).astype(jnp.bfloat16)
    wide_rows = stream.astype(jnp.float32)
    squares = lax.optimization_barrier(jnp.sum(wide_rows * wide_rows, axis=1))
    inverse = lax.rsqrt(squares / D + 1e-06)
    normed = (wide_rows * inverse[:, None] * norm_gain.astype(jnp.float32)[None, :]).astype(jnp.bfloat16)
    gate_acts = jnp.dot(normed, gate_w, preferred_element_type=jnp.float32)
    up_acts = jnp.dot(normed, up_w, preferred_element_type=jnp.float32)
    hidden = (jax.nn.silu(gate_acts) * up_acts).astype(jnp.bfloat16)
    summed = jnp.dot(hidden, down_w, preferred_element_type=jnp.float32)
    return (wide_rows + summed).astype(jnp.bfloat16)
```

```python
import functools
import math

import jax
import jax.numpy as jnp
from jax import lax
from jax.experimental import pallas as pl
from jax.experimental.pallas import tpu as pltpu
from jax.sharding import PartitionSpec as P

HD = 128
G = 5


CORES = 2
EPS = 1e-06


def remote(src, dst, send_sem, recv_sem, target):
    return pltpu.make_async_remote_copy(
        src_ref=src,
        dst_ref=dst,
        send_sem=send_sem,
        recv_sem=recv_sem,
        device_id={"shard": target},
        device_id_type=pl.DeviceIdType.MESH,
    )


def layer_kernel(
    shards,
    requests,
    drafts,
    attn_ref,
    resid_ref,
    gain_ref,
    wo_hbm,
    gate_hbm,
    up_hbm,
    down_hbm,
    out_ref,
    wo,
    gate,
    up,
    down,
    attn_slots,
    gain_slots,
    stream_slots,
    low_rows,
    wide_rows,
    own_rows,
    gains,
    hidden,
    mine_block,
    other_block,
    pair_out,
    pair_in,
    send_blocks,
    recv_blocks,
    weight_sems,
    attn_sems,
    gain_sems,
    stream_sems,
    pair_sems,
    final_sems,
):
    chips = shards // CORES
    me = lax.axis_index("shard")
    chip = me // CORES
    core = me % CORES
    pair = chip * CORES + 1 - core
    rows, depth = low_rows.shape
    width = resid_ref.shape[1]
    out_rows = out_ref.shape[0]
    pieces = down.shape[0]
    total_pieces = depth // down.shape[2]
    piece = down.shape[2]
    chip_rows = out_rows * CORES

    def down_copy(q):
        return pltpu.make_async_copy(
            down_hbm.at[:, pl.ds(q * piece, piece)], down.at[q % pieces], weight_sems.at[3 + q]
        )

    wo_copy = pltpu.make_async_copy(wo_hbm, wo, weight_sems.at[0])
    gate_copy = pltpu.make_async_copy(gate_hbm, gate, weight_sems.at[1])
    up_copy = pltpu.make_async_copy(up_hbm, up, weight_sems.at[2])
    wo_copy.start()
    gate_copy.start()
    up_copy.start()
    for q in range(pieces):
        down_copy(q).start()

    barrier = pltpu.get_barrier_semaphore()

    def greet(j, carry):
        target = ((chip + j) % chips) * CORES + core
        pl.semaphore_signal(
            barrier, inc=1, device_id={"shard": target}, device_id_type=pl.DeviceIdType.MESH
        )
        return carry

    lax.fori_loop(1, chips, greet, 0)
    pl.semaphore_signal(
        barrier, inc=1, device_id={"shard": pair}, device_id_type=pl.DeviceIdType.MESH
    )
    pl.semaphore_wait(barrier, chips)

    def direct(slots, sems, j):
        target = ((chip + j) % chips) * CORES + core
        return remote(slots.at[me], slots.at[me], sems.at[0, j], sems.at[1, chip], target)

    def relay(slots, sems, j):
        origin = (chip + chips - j) % chips
        block = origin * CORES + core
        return remote(slots.at[block], slots.at[block], sems.at[2, j], sems.at[3, origin], pair)

    def gather_start(slots, sems):
        def send(j, carry):
            direct(slots, sems, j).start()
            return carry

        relay(slots, sems, 0).start()
        lax.fori_loop(1, chips, send, 0)

    def gather_finish(slots, sems):
        def forward(j, carry):
            origin = (chip + chips - j) % chips
            block = origin * CORES + core
            remote(
                slots.at[block], slots.at[block], sems.at[0, j], sems.at[1, origin], pair
            ).wait_recv()
            relay(slots, sems, j).start()
            return carry

        def arrive(j, carry):
            origin = (chip + chips - j) % chips
            block = origin * CORES + 1 - core
            remote(
                slots.at[block], slots.at[block], sems.at[2, j], sems.at[3, origin], pair
            ).wait_recv()
            return carry

        lax.fori_loop(1, chips, forward, 0)
        lax.fori_loop(0, chips, arrive, 0)

    def gather_drain(slots, sems):
        def drain(j, carry):
            direct(slots, sems, j).wait_send()
            relay(slots, sems, j).wait_send()
            return carry

        relay(slots, sems, 0).wait_send()
        lax.fori_loop(1, chips, drain, 0)

    attn_slots[me] = attn_ref[...]
    gain_slots[me] = gain_ref[...]
    gather_start(attn_slots, attn_sems)
    gather_start(gain_slots, gain_sems)
    gather_finish(attn_slots, attn_sems)

    blocks = attn_ref.shape[0] // drafts
    head_width = attn_ref.shape[1]
    for p in range(shards * blocks):
        head, request = p // requests, p % requests
        low_rows[
            request * drafts : (request + 1) * drafts, head * head_width : (head + 1) * head_width
        ] = attn_slots[p // blocks, (p % blocks) * drafts : (p % blocks + 1) * drafts, :]
    wo_copy.wait()
    mixed = jnp.dot(low_rows[...], wo[...], preferred_element_type=jnp.float32)
    stream_slots[me] = (resid_ref[...].astype(jnp.float32) + mixed).astype(jnp.bfloat16)
    gather_start(stream_slots, stream_sems)
    gather_finish(gain_slots, gain_sems)
    for s in range(shards):
        gains[:, s * width : (s + 1) * width] = gain_slots[s]
    gather_finish(stream_slots, stream_sems)
    for s in range(shards):
        wide_rows[:, s * width : (s + 1) * width] = stream_slots[s].astype(jnp.float32)
    own_rows[...] = wide_rows[pl.ds(pl.multiple_of(chip * chip_rows, chip_rows), chip_rows), :]

    def norm(i, carry):
        band = pl.ds(pl.multiple_of(i * 16, 16), 16)
        wide = wide_rows[band, :]
        inverse = lax.rsqrt(jnp.sum(wide * wide, axis=1, keepdims=True) / depth + EPS)
        low_rows[band, :] = (wide * inverse * gains[...]).astype(jnp.bfloat16)
        return carry

    lax.fori_loop(0, rows // 16, norm, 0)

    gate_copy.wait()
    up_copy.wait()
    units = gate.shape[1]
    for first in range(0, units, 512):
        last = min(first + 512, units)
        gate_acts = jnp.dot(
            low_rows[...], gate[:, first:last], preferred_element_type=jnp.float32
        )
        up_acts = jnp.dot(low_rows[...], up[:, first:last], preferred_element_type=jnp.float32)
        hidden[:, first:last] = (jax.nn.silu(gate_acts) * up_acts).astype(jnp.bfloat16)

    for q in range(total_pieces):
        down_copy(q).wait()
        wide_rows[:, q * piece : (q + 1) * piece] = jnp.dot(
            hidden[...], down[q % pieces], preferred_element_type=jnp.float32
        )
        if q + pieces < total_pieces:
            down_copy(q + pieces).start()

    def take(c, block, which):
        for q in range(total_pieces):
            both = wide_rows[
                pl.ds(pl.multiple_of(c * chip_rows, chip_rows), chip_rows),
                q * piece : (q + 1) * piece,
            ]
            block[q * out_rows : (q + 1) * out_rows, :] = jnp.where(
                which == 0, both[:out_rows], both[out_rows:]
            )
        return block[...]

    def give(c, carry):
        pair_out[c] = take(c, other_block, 1 - core).astype(jnp.bfloat16)
        return carry

    lax.fori_loop(0, chips, give, 0)
    pair_copy = remote(pair_out, pair_in, pair_sems.at[0], pair_sems.at[1], pair)
    pair_copy.start()
    pair_copy.wait()

    def scatter(j):
        target = (chip + j) % chips
        return remote(
            send_blocks.at[target],
            recv_blocks.at[chip],
            final_sems.at[0, j],
            final_sems.at[1, chip],
            target * CORES + core,
        )

    def combine(j, carry):
        target = (chip + j) % chips
        summed = take(target, mine_block, core) + pair_in[target].astype(jnp.float32)
        send_blocks[target] = summed.astype(jnp.bfloat16)
        scatter(j).start()
        return carry

    lax.fori_loop(1, chips, combine, 0)
    total = take(chip, mine_block, core) + pair_in[chip].astype(jnp.float32)

    def add(j, total):
        origin = (chip + chips - j) % chips
        remote(
            send_blocks.at[origin],
            recv_blocks.at[origin],
            final_sems.at[0, j],
            final_sems.at[1, origin],
            pair,
        ).wait_recv()
        return total + recv_blocks[origin].astype(jnp.float32)

    mine_block[...] = lax.fori_loop(1, chips, add, total)
    for q in range(total_pieces):
        both = own_rows[:, q * piece : (q + 1) * piece]
        stream = jnp.where(core == 0, both[:out_rows], both[out_rows:])
        out_ref[:, q * piece : (q + 1) * piece] = (
            stream + mine_block[q * out_rows : (q + 1) * out_rows, :]
        ).astype(jnp.bfloat16)

    def drain(j, carry):
        scatter(j).wait_send()
        return carry

    lax.fori_loop(1, chips, drain, 0)
    gather_drain(attn_slots, attn_sems)
    gather_drain(gain_slots, gain_sems)
    gather_drain(stream_slots, stream_sems)


def rest_of_layer(shards, requests, drafts, attn, residual_in, norm_gain, *weights):
    rows, width = residual_in.shape
    out_proj, gate_w, up_w, down_w = weights
    depth = out_proj.shape[0]
    units = gate_w.shape[1]
    chips = shards // CORES
    out_rows = rows // shards
    piece = depth * out_rows // 16
    slots = (chips, 16, piece)
    bf16, f32 = jnp.bfloat16, jnp.float32
    vmem, hbm = pl.BlockSpec(memory_space=pltpu.VMEM), pl.BlockSpec(memory_space=pl.ANY)
    dma = pltpu.SemaphoreType.DMA
    return pl.pallas_call(
        functools.partial(layer_kernel, shards, requests, drafts),
        out_shape=jax.ShapeDtypeStruct((out_rows, depth), bf16),
        in_specs=[vmem] * 3 + [hbm] * 4,
        out_specs=vmem,
        scratch_shapes=[
            pltpu.VMEM(out_proj.shape, bf16),
            pltpu.VMEM(gate_w.shape, bf16),
            pltpu.VMEM(up_w.shape, bf16),
            pltpu.VMEM((2, units, piece), bf16),
            pltpu.VMEM((shards,) + attn.shape, bf16),
            pltpu.VMEM((shards, 1, width), f32),
            pltpu.VMEM((shards, rows, width), bf16),
            pltpu.VMEM((rows, depth), bf16),
            pltpu.VMEM((rows, depth), f32),
            pltpu.VMEM((CORES * out_rows, depth), f32),
            pltpu.VMEM((1, depth), f32),
            pltpu.VMEM((rows, units), bf16),
            pltpu.VMEM((16, piece), f32),
            pltpu.VMEM((16, piece), f32),
            pltpu.VMEM(slots, bf16),
            pltpu.VMEM(slots, bf16),
            pltpu.VMEM(slots, bf16),
            pltpu.VMEM(slots, bf16),
            dma((3 + depth // piece,)),
            dma((4, chips)),
            dma((4, chips)),
            dma((4, chips)),
            dma((2,)),
            dma((2, chips)),
        ],
        compiler_params=pltpu.CompilerParams(
            collective_id=0, has_side_effects=True, vmem_limit_bytes=60 * 1024 * 1024
        ),
        cost_estimate=pl.CostEstimate(
            flops=2 * rows * (depth * width + 3 * depth * units),
            bytes_accessed=2 * (depth * width + 3 * depth * units),
            transcendentals=rows * units,
        ),
    )(attn, residual_in, norm_gain.astype(f32).reshape(1, width), *weights)

def on_device(
    shards,
    residual_in,
    queries,
    key_cache,
    value_cache,
    new_keys,
    new_values,
    cache_len,
    tree_mask,
    out_proj,
    norm_gain,
    gate_w,
    up_w,
    down_w,
):
    blocks = queries.shape[0]
    drafts = queries.shape[1]
    requests = cache_len.shape[0]
    first_pair = lax.axis_index("shard") * blocks
    pair_index = first_pair + jnp.arange(blocks, dtype=jnp.int32)
    req_index = pair_index % requests
    req_pick = (req_index[:, None] == jnp.arange(requests, dtype=jnp.int32)[None, :]).astype(
        jnp.int32
    )
    lengths = jnp.sum(req_pick * cache_len[None, :], axis=1)
    tree_rows = jnp.einsum("br,rij->bij", req_pick, tree_mask)
    head_rows = queries.reshape(blocks, drafts, G, HD)
    score_scale = 1.0 / math.sqrt(HD)
    cache_scores = (
        jnp.einsum("bdgk,blk->bdgl", head_rows, key_cache, preferred_element_type=jnp.float32)
        * score_scale
    )
    draft_scores = (
        jnp.einsum("bdgk,bek->bdge", head_rows, new_keys, preferred_element_type=jnp.float32)
        * score_scale
    )
    valid_keys = jnp.arange(key_cache.shape[1], dtype=jnp.int32)[None, :] < lengths[:, None]
    cache_scores = jnp.where(valid_keys[:, None, None, :], cache_scores, -1e30)
    draft_scores = jnp.where(tree_rows[:, :, None, :] > 0, draft_scores, -1e30)
    peak_score = jnp.maximum(jnp.max(cache_scores, axis=-1), jnp.max(draft_scores, axis=-1))
    cache_weights = jnp.where(
        valid_keys[:, None, None, :], jnp.exp(cache_scores - peak_score[..., None]), 0.0
    )
    draft_weights = jnp.where(
        tree_rows[:, :, None, :] > 0, jnp.exp(draft_scores - peak_score[..., None]), 0.0
    )
    denom = jnp.sum(cache_weights, axis=-1) + jnp.sum(draft_weights, axis=-1)
    weighted = jnp.einsum(
        "bdgl,blk->bdgk",
        cache_weights.astype(jnp.bfloat16),
        value_cache,
        preferred_element_type=jnp.float32,
    )
    weighted = weighted + jnp.einsum(
        "bdge,bek->bdgk",
        draft_weights.astype(jnp.bfloat16),
        new_values,
        preferred_element_type=jnp.float32,
    )
    attn = (weighted / denom[..., None]).astype(jnp.bfloat16).reshape(blocks, drafts, G * HD)
    return rest_of_layer(
        shards,
        requests,
        drafts,
        attn.reshape(blocks * drafts, G * HD),
        residual_in,
        norm_gain,
        out_proj,
        gate_w,
        up_w,
        down_w,
    )


def solution(mesh):
    placed = (
        P("groups", "shard"),
        P(("groups", "shard"), None, None),
        P(("groups", "shard"), None, None),
        P(("groups", "shard"), None, None),
        P(("groups", "shard"), None, None),
        P(("groups", "shard"), None, None),
        P("groups"),
        P("groups", None, None),
        P(None, "shard"),
        P("shard"),
        P(None, "shard"),
        P(None, "shard"),
        P("shard", None),
    )
    return jax.shard_map(
        functools.partial(on_device, mesh.shape["shard"]),
        mesh=mesh,
        in_specs=placed,
        out_specs=P(("groups", "shard"), None),
        check_vma=False,
    )
```

```python
import functools
import math

import jax
import jax.numpy as jnp
from jax import lax
from jax.experimental import pallas as pl
from jax.experimental.pallas import tpu as pltpu
from jax.sharding import PartitionSpec as P

HD = 128
G = 5


CORES = 2
EPS = 1e-06


def remote(src, dst, send_sem, recv_sem, target):
    return pltpu.make_async_remote_copy(
        src_ref=src,
        dst_ref=dst,
        send_sem=send_sem,
        recv_sem=recv_sem,
        device_id={"shard": target},
        device_id_type=pl.DeviceIdType.MESH,
    )


def dot_transposed(a, b):
    return lax.dot_general(a, b, (((1,), (1,)), ((), ())), preferred_element_type=jnp.float32)


def layer_kernel(
    shards,
    requests,
    drafts,
    attn_ref,
    resid_ref,
    gain_ref,
    wo_hbm,
    gate_hbm,
    up_hbm,
    down_hbm,
    out_ref,
    wo,
    gate,
    up,
    down,
    attn_slots,
    gain_slots,
    stream_slots,
    low_rows,
    wide_rows,
    own_rows,
    gains,
    hidden,
    mine_block,
    other_block,
    pair_out,
    pair_in,
    send_blocks,
    recv_blocks,
    weight_sems,
    attn_sems,
    gain_sems,
    stream_sems,
    pair_sems,
    final_sems,
):
    chips = shards // CORES
    me = lax.axis_index("shard")
    chip = me // CORES
    core = me % CORES
    pair = chip * CORES + 1 - core
    rows, depth = low_rows.shape
    width = resid_ref.shape[1]
    out_rows = out_ref.shape[0]
    pieces = down.shape[0]
    total_pieces = depth // down.shape[2]
    piece = down.shape[2]
    chip_rows = out_rows * CORES

    def down_copy(q):
        return pltpu.make_async_copy(
            down_hbm.at[:, pl.ds(q * piece, piece)], down.at[q % pieces], weight_sems.at[3 + q]
        )

    wo_copy = pltpu.make_async_copy(wo_hbm, wo, weight_sems.at[0])
    gate_copy = pltpu.make_async_copy(gate_hbm, gate, weight_sems.at[1])
    up_copy = pltpu.make_async_copy(up_hbm, up, weight_sems.at[2])
    wo_copy.start()
    gate_copy.start()
    up_copy.start()
    for q in range(pieces):
        down_copy(q).start()

    barrier = pltpu.get_barrier_semaphore()

    def greet(j, carry):
        target = ((chip + j) % chips) * CORES + core
        pl.semaphore_signal(
            barrier, inc=1, device_id={"shard": target}, device_id_type=pl.DeviceIdType.MESH
        )
        return carry

    lax.fori_loop(1, chips, greet, 0)
    pl.semaphore_signal(
        barrier, inc=1, device_id={"shard": pair}, device_id_type=pl.DeviceIdType.MESH
    )
    pl.semaphore_wait(barrier, chips)

    def direct(slots, sems, j):
        target = ((chip + j) % chips) * CORES + core
        return remote(slots.at[me], slots.at[me], sems.at[0, j], sems.at[1, chip], target)

    def relay(slots, sems, j):
        origin = (chip + chips - j) % chips
        block = origin * CORES + core
        return remote(slots.at[block], slots.at[block], sems.at[2, j], sems.at[3, origin], pair)

    def gather_start(slots, sems):
        def send(j, carry):
            direct(slots, sems, j).start()
            return carry

        relay(slots, sems, 0).start()
        lax.fori_loop(1, chips, send, 0)

    def gather_finish(slots, sems):
        def forward(j, carry):
            origin = (chip + chips - j) % chips
            block = origin * CORES + core
            remote(
                slots.at[block], slots.at[block], sems.at[0, j], sems.at[1, origin], pair
            ).wait_recv()
            relay(slots, sems, j).start()
            return carry

        def arrive(j, carry):
            origin = (chip + chips - j) % chips
            block = origin * CORES + 1 - core
            remote(
                slots.at[block], slots.at[block], sems.at[2, j], sems.at[3, origin], pair
            ).wait_recv()
            return carry

        lax.fori_loop(1, chips, forward, 0)
        lax.fori_loop(0, chips, arrive, 0)

    def gather_drain(slots, sems):
        def drain(j, carry):
            direct(slots, sems, j).wait_send()
            relay(slots, sems, j).wait_send()
            return carry

        relay(slots, sems, 0).wait_send()
        lax.fori_loop(1, chips, drain, 0)

    attn_slots[me] = attn_ref[...]
    gain_slots[me] = gain_ref[...]
    gather_start(attn_slots, attn_sems)
    gather_start(gain_slots, gain_sems)
    gather_finish(attn_slots, attn_sems)

    blocks = attn_ref.shape[0] // drafts
    head_width = attn_ref.shape[1]
    for p in range(shards * blocks):
        head, request = p // requests, p % requests
        low_rows[
            request * drafts : (request + 1) * drafts, head * head_width : (head + 1) * head_width
        ] = attn_slots[p // blocks, (p % blocks) * drafts : (p % blocks + 1) * drafts, :]
    wo_copy.wait()
    mixed = dot_transposed(low_rows[...], wo[...])
    stream_slots[me] = (resid_ref[...].astype(jnp.float32) + mixed).astype(jnp.bfloat16)
    gather_start(stream_slots, stream_sems)
    gather_finish(gain_slots, gain_sems)
    for s in range(shards):
        gains[:, s * width : (s + 1) * width] = gain_slots[s]
    gather_finish(stream_slots, stream_sems)
    for s in range(shards):
        wide_rows[:, s * width : (s + 1) * width] = stream_slots[s].astype(jnp.float32)
    own_rows[...] = wide_rows[pl.ds(pl.multiple_of(chip * chip_rows, chip_rows), chip_rows), :]

    def norm(i, carry):
        band = pl.ds(pl.multiple_of(i * 16, 16), 16)
        wide = wide_rows[band, :]
        inverse = lax.rsqrt(jnp.sum(wide * wide, axis=1, keepdims=True) / depth + EPS)
        low_rows[band, :] = (wide * inverse * gains[...]).astype(jnp.bfloat16)
        return carry

    lax.fori_loop(0, rows // 16, norm, 0)

    gate_copy.wait()
    up_copy.wait()
    units = gate.shape[0]
    for first in range(0, units, 512):
        last = min(first + 512, units)
        gate_acts = dot_transposed(low_rows[...], gate[first:last, :])
        up_acts = dot_transposed(low_rows[...], up[first:last, :])
        hidden[:, first:last] = (jax.nn.silu(gate_acts) * up_acts).astype(jnp.bfloat16)

    for q in range(total_pieces):
        down_copy(q).wait()
        wide_rows[:, q * piece : (q + 1) * piece] = jnp.dot(
            hidden[...], down[q % pieces], preferred_element_type=jnp.float32
        )
        if q + pieces < total_pieces:
            down_copy(q + pieces).start()

    def take(c, block, which):
        for q in range(total_pieces):
            both = wide_rows[
                pl.ds(pl.multiple_of(c * chip_rows, chip_rows), chip_rows),
                q * piece : (q + 1) * piece,
            ]
            block[q * out_rows : (q + 1) * out_rows, :] = jnp.where(
                which == 0, both[:out_rows], both[out_rows:]
            )
        return block[...]

    def give(c, carry):
        pair_out[c] = take(c, other_block, 1 - core).astype(jnp.bfloat16)
        return carry

    lax.fori_loop(0, chips, give, 0)
    pair_copy = remote(pair_out, pair_in, pair_sems.at[0], pair_sems.at[1], pair)
    pair_copy.start()
    pair_copy.wait()

    def scatter(j):
        target = (chip + j) % chips
        return remote(
            send_blocks.at[target],
            recv_blocks.at[chip],
            final_sems.at[0, j],
            final_sems.at[1, chip],
            target * CORES + core,
        )

    def combine(j, carry):
        target = (chip + j) % chips
        summed = take(target, mine_block, core) + pair_in[target].astype(jnp.float32)
        send_blocks[target] = summed.astype(jnp.bfloat16)
        scatter(j).start()
        return carry

    lax.fori_loop(1, chips, combine, 0)
    total = take(chip, mine_block, core) + pair_in[chip].astype(jnp.float32)

    def add(j, total):
        origin = (chip + chips - j) % chips
        remote(
            send_blocks.at[origin],
            recv_blocks.at[origin],
            final_sems.at[0, j],
            final_sems.at[1, origin],
            pair,
        ).wait_recv()
        return total + recv_blocks[origin].astype(jnp.float32)

    mine_block[...] = lax.fori_loop(1, chips, add, total)
    for q in range(total_pieces):
        both = own_rows[:, q * piece : (q + 1) * piece]
        stream = jnp.where(core == 0, both[:out_rows], both[out_rows:])
        out_ref[:, q * piece : (q + 1) * piece] = (
            stream + mine_block[q * out_rows : (q + 1) * out_rows, :]
        ).astype(jnp.bfloat16)

    def drain(j, carry):
        scatter(j).wait_send()
        return carry

    lax.fori_loop(1, chips, drain, 0)
    gather_drain(attn_slots, attn_sems)
    gather_drain(gain_slots, gain_sems)
    gather_drain(stream_slots, stream_sems)


def rest_of_layer(shards, requests, drafts, attn, residual_in, norm_gain, *weights):
    rows, width = residual_in.shape
    out_proj, gate_w, up_w, down_w = weights
    depth = out_proj.shape[1]
    units = gate_w.shape[0]
    chips = shards // CORES
    out_rows = rows // shards
    piece = depth * out_rows // 16
    slots = (chips, 16, piece)
    bf16, f32 = jnp.bfloat16, jnp.float32
    vmem, hbm = pl.BlockSpec(memory_space=pltpu.VMEM), pl.BlockSpec(memory_space=pl.ANY)
    dma = pltpu.SemaphoreType.DMA
    return pl.pallas_call(
        functools.partial(layer_kernel, shards, requests, drafts),
        out_shape=jax.ShapeDtypeStruct((out_rows, depth), bf16),
        in_specs=[vmem] * 3 + [hbm] * 4,
        out_specs=vmem,
        scratch_shapes=[
            pltpu.VMEM(out_proj.shape, bf16),
            pltpu.VMEM(gate_w.shape, bf16),
            pltpu.VMEM(up_w.shape, bf16),
            pltpu.VMEM((2, units, piece), bf16),
            pltpu.VMEM((shards,) + attn.shape, bf16),
            pltpu.VMEM((shards, 1, width), f32),
            pltpu.VMEM((shards, rows, width), bf16),
            pltpu.VMEM((rows, depth), bf16),
            pltpu.VMEM((rows, depth), f32),
            pltpu.VMEM((CORES * out_rows, depth), f32),
            pltpu.VMEM((1, depth), f32),
            pltpu.VMEM((rows, units), bf16),
            pltpu.VMEM((16, piece), f32),
            pltpu.VMEM((16, piece), f32),
            pltpu.VMEM(slots, bf16),
            pltpu.VMEM(slots, bf16),
            pltpu.VMEM(slots, bf16),
            pltpu.VMEM(slots, bf16),
            dma((3 + depth // piece,)),
            dma((4, chips)),
            dma((4, chips)),
            dma((4, chips)),
            dma((2,)),
            dma((2, chips)),
        ],
        compiler_params=pltpu.CompilerParams(
            collective_id=0, has_side_effects=True, vmem_limit_bytes=60 * 1024 * 1024
        ),
        cost_estimate=pl.CostEstimate(
            flops=2 * rows * (depth * width + 3 * depth * units),
            bytes_accessed=2 * (depth * width + 3 * depth * units),
            transcendentals=rows * units,
        ),
    )(attn, residual_in, norm_gain.astype(f32).reshape(1, width), *weights)

def on_device(
    shards,
    residual_in,
    queries,
    key_cache,
    value_cache,
    new_keys,
    new_values,
    cache_len,
    tree_mask,
    out_proj,
    norm_gain,
    gate_w,
    up_w,
    down_w,
):
    blocks = queries.shape[0]
    drafts = queries.shape[1]
    requests = cache_len.shape[0]
    first_pair = lax.axis_index("shard") * blocks
    pair_index = first_pair + jnp.arange(blocks, dtype=jnp.int32)
    req_index = pair_index % requests
    req_pick = (req_index[:, None] == jnp.arange(requests, dtype=jnp.int32)[None, :]).astype(
        jnp.int32
    )
    lengths = jnp.sum(req_pick * cache_len[None, :], axis=1)
    tree_rows = jnp.einsum("br,rij->bij", req_pick, tree_mask)
    head_rows = queries.reshape(blocks, drafts, G, HD)
    score_scale = 1.0 / math.sqrt(HD)
    cache_scores = (
        jnp.einsum("bdgk,blk->bdgl", head_rows, key_cache, preferred_element_type=jnp.float32)
        * score_scale
    )
    draft_scores = (
        jnp.einsum("bdgk,bek->bdge", head_rows, new_keys, preferred_element_type=jnp.float32)
        * score_scale
    )
    valid_keys = jnp.arange(key_cache.shape[1], dtype=jnp.int32)[None, :] < lengths[:, None]
    cache_scores = jnp.where(valid_keys[:, None, None, :], cache_scores, -1e30)
    draft_scores = jnp.where(tree_rows[:, :, None, :] > 0, draft_scores, -1e30)
    peak_score = jnp.maximum(jnp.max(cache_scores, axis=-1), jnp.max(draft_scores, axis=-1))
    cache_weights = jnp.where(
        valid_keys[:, None, None, :], jnp.exp(cache_scores - peak_score[..., None]), 0.0
    )
    draft_weights = jnp.where(
        tree_rows[:, :, None, :] > 0, jnp.exp(draft_scores - peak_score[..., None]), 0.0
    )
    denom = jnp.sum(cache_weights, axis=-1) + jnp.sum(draft_weights, axis=-1)
    weighted = jnp.einsum(
        "bdgl,blk->bdgk",
        cache_weights.astype(jnp.bfloat16),
        value_cache,
        preferred_element_type=jnp.float32,
    )
    weighted = weighted + jnp.einsum(
        "bdge,bek->bdgk",
        draft_weights.astype(jnp.bfloat16),
        new_values,
        preferred_element_type=jnp.float32,
    )
    attn = (weighted / denom[..., None]).astype(jnp.bfloat16).reshape(blocks, drafts, G * HD)
    return rest_of_layer(
        shards,
        requests,
        drafts,
        attn.reshape(blocks * drafts, G * HD),
        residual_in,
        norm_gain,
        out_proj.T,
        gate_w.T,
        up_w.T,
        down_w,
    )


def solution(mesh):
    placed = (
        P("groups", "shard"),
        P(("groups", "shard"), None, None),
        P(("groups", "shard"), None, None),
        P(("groups", "shard"), None, None),
        P(("groups", "shard"), None, None),
        P(("groups", "shard"), None, None),
        P("groups"),
        P("groups", None, None),
        P(None, "shard"),
        P("shard"),
        P(None, "shard"),
        P(None, "shard"),
        P("shard", None),
    )
    return jax.shard_map(
        functools.partial(on_device, mesh.shape["shard"]),
        mesh=mesh,
        in_specs=placed,
        out_specs=P(("groups", "shard"), None),
        check_vma=False,
    )
```

```python
import functools
import math

import jax
import jax.numpy as jnp
from jax import lax
from jax.experimental import pallas as pl
from jax.experimental.pallas import tpu as pltpu
from jax.sharding import PartitionSpec as P

HD = 128
G = 5


CORES = 2
EPS = 1e-06


def remote(src, dst, send_sem, recv_sem, target):
    return pltpu.make_async_remote_copy(
        src_ref=src,
        dst_ref=dst,
        send_sem=send_sem,
        recv_sem=recv_sem,
        device_id={"shard": target},
        device_id_type=pl.DeviceIdType.MESH,
    )


def dot_transposed(a, b):
    return lax.dot_general(a, b, (((1,), (1,)), ((), ())), preferred_element_type=jnp.float32)


def layer_kernel(
    shards,
    requests,
    drafts,
    attn_ref,
    resid_ref,
    gain_ref,
    wo_hbm,
    gate_hbm,
    up_hbm,
    down_hbm,
    out_ref,
    wo,
    gate,
    up,
    down,
    attn_slots,
    gain_slots,
    stream_slots,
    low_rows,
    wide_rows,
    own_rows,
    gains,
    hidden,
    mine_block,
    other_block,
    pair_out,
    pair_in,
    send_blocks,
    recv_blocks,
    weight_sems,
    attn_sems,
    gain_sems,
    stream_sems,
    pair_sems,
    final_sems,
):
    chips = shards // CORES
    me = lax.axis_index("shard")
    chip = me // CORES
    core = me % CORES
    pair = chip * CORES + 1 - core
    rows, depth = low_rows.shape
    width = resid_ref.shape[1]
    out_rows = out_ref.shape[0]
    pieces = down.shape[0]
    total_pieces = depth // down.shape[2]
    piece = down.shape[2]
    chip_rows = out_rows * CORES

    def down_copy(q):
        return pltpu.make_async_copy(
            down_hbm.at[:, pl.ds(q * piece, piece)], down.at[q % pieces], weight_sems.at[3 + q]
        )

    wo_copy = pltpu.make_async_copy(wo_hbm, wo, weight_sems.at[0])
    gate_copy = pltpu.make_async_copy(gate_hbm, gate, weight_sems.at[1])
    up_copy = pltpu.make_async_copy(up_hbm, up, weight_sems.at[2])
    wo_copy.start()
    gate_copy.start()
    up_copy.start()
    for q in range(pieces):
        down_copy(q).start()

    barrier = pltpu.get_barrier_semaphore()

    def greet(j, carry):
        target = ((chip + j) % chips) * CORES + core
        pl.semaphore_signal(
            barrier, inc=1, device_id={"shard": target}, device_id_type=pl.DeviceIdType.MESH
        )
        return carry

    lax.fori_loop(1, chips, greet, 0)
    pl.semaphore_signal(
        barrier, inc=1, device_id={"shard": pair}, device_id_type=pl.DeviceIdType.MESH
    )
    pl.semaphore_wait(barrier, chips)

    def direct(slots, sems, j):
        target = ((chip + j) % chips) * CORES + core
        return remote(slots.at[me], slots.at[me], sems.at[0, j], sems.at[1, chip], target)

    def relay(slots, sems, j):
        origin = (chip + chips - j) % chips
        block = origin * CORES + core
        return remote(slots.at[block], slots.at[block], sems.at[2, j], sems.at[3, origin], pair)

    def gather_start(slots, sems):
        def send(j, carry):
            direct(slots, sems, j).start()
            return carry

        relay(slots, sems, 0).start()
        lax.fori_loop(1, chips, send, 0)

    def gather_finish(slots, sems):
        def forward(j, carry):
            origin = (chip + chips - j) % chips
            block = origin * CORES + core
            remote(
                slots.at[block], slots.at[block], sems.at[0, j], sems.at[1, origin], pair
            ).wait_recv()
            relay(slots, sems, j).start()
            return carry

        def arrive(j, carry):
            origin = (chip + chips - j) % chips
            block = origin * CORES + 1 - core
            remote(
                slots.at[block], slots.at[block], sems.at[2, j], sems.at[3, origin], pair
            ).wait_recv()
            return carry

        lax.fori_loop(1, chips, forward, 0)
        lax.fori_loop(0, chips, arrive, 0)

    def gather_drain(slots, sems):
        def drain(j, carry):
            direct(slots, sems, j).wait_send()
            relay(slots, sems, j).wait_send()
            return carry

        relay(slots, sems, 0).wait_send()
        lax.fori_loop(1, chips, drain, 0)

    attn_slots[me] = attn_ref[...]
    gain_slots[me] = gain_ref[...]
    gather_start(attn_slots, attn_sems)
    gather_start(gain_slots, gain_sems)
    gather_finish(attn_slots, attn_sems)

    blocks = attn_ref.shape[0] // drafts
    head_width = attn_ref.shape[1]
    for p in range(shards * blocks):
        head, request = p // requests, p % requests
        low_rows[
            request * drafts : (request + 1) * drafts, head * head_width : (head + 1) * head_width
        ] = attn_slots[p // blocks, (p % blocks) * drafts : (p % blocks + 1) * drafts, :]
    wo_copy.wait()
    mixed = dot_transposed(low_rows[...], wo[...])
    stream_slots[me] = (resid_ref[...].astype(jnp.float32) + mixed).astype(jnp.bfloat16)
    gather_start(stream_slots, stream_sems)
    gather_finish(gain_slots, gain_sems)
    for s in range(shards):
        gains[:, s * width : (s + 1) * width] = gain_slots[s]
    gather_finish(stream_slots, stream_sems)
    for s in range(shards):
        wide_rows[:, s * width : (s + 1) * width] = stream_slots[s].astype(jnp.float32)
    own_rows[...] = wide_rows[pl.ds(pl.multiple_of(chip * chip_rows, chip_rows), chip_rows), :]

    def norm(i, carry):
        band = pl.ds(pl.multiple_of(i * 16, 16), 16)
        wide = wide_rows[band, :]
        inverse = lax.rsqrt(jnp.sum(wide * wide, axis=1, keepdims=True) / depth + EPS)
        low_rows[band, :] = (wide * inverse * gains[...]).astype(jnp.bfloat16)
        return carry

    lax.fori_loop(0, rows // 16, norm, 0)

    gate_copy.wait()
    up_copy.wait()
    units = gate.shape[0]
    for first in range(0, units, 512):
        last = min(first + 512, units)
        gate_acts = dot_transposed(low_rows[...], gate[first:last, :])
        up_acts = dot_transposed(low_rows[...], up[first:last, :])
        hidden[:, first:last] = (jax.nn.silu(gate_acts) * up_acts).astype(jnp.bfloat16)

    for q in range(total_pieces):
        down_copy(q).wait()
        wide_rows[:, q * piece : (q + 1) * piece] = jnp.dot(
            hidden[...], down[q % pieces], preferred_element_type=jnp.float32
        )
        if q + pieces < total_pieces:
            down_copy(q + pieces).start()

    def take(c, block, which):
        for q in range(total_pieces):
            both = wide_rows[
                pl.ds(pl.multiple_of(c * chip_rows, chip_rows), chip_rows),
                q * piece : (q + 1) * piece,
            ]
            block[q * out_rows : (q + 1) * out_rows, :] = jnp.where(
                which == 0, both[:out_rows], both[out_rows:]
            )
        return block[...]

    def exchange(c):
        return remote(pair_out.at[c], pair_in.at[c], pair_sems.at[0, c], pair_sems.at[1, c], pair)

    def give(j, carry):
        c = (chip + j) % chips
        pair_out[c] = take(c, other_block, 1 - core).astype(jnp.bfloat16)
        exchange(c).start()
        return carry

    lax.fori_loop(1, chips + 1, give, 0)

    def scatter(j):
        target = (chip + j) % chips
        return remote(
            send_blocks.at[target],
            recv_blocks.at[chip],
            final_sems.at[0, j],
            final_sems.at[1, chip],
            target * CORES + core,
        )

    def combine(j, carry):
        target = (chip + j) % chips
        exchange(target).wait_recv()
        summed = take(target, mine_block, core) + pair_in[target].astype(jnp.float32)
        send_blocks[target] = summed.astype(jnp.bfloat16)
        scatter(j).start()
        return carry

    lax.fori_loop(1, chips, combine, 0)
    exchange(chip).wait_recv()
    total = take(chip, mine_block, core) + pair_in[chip].astype(jnp.float32)

    def add(j, total):
        origin = (chip + chips - j) % chips
        remote(
            send_blocks.at[origin],
            recv_blocks.at[origin],
            final_sems.at[0, j],
            final_sems.at[1, origin],
            pair,
        ).wait_recv()
        return total + recv_blocks[origin].astype(jnp.float32)

    mine_block[...] = lax.fori_loop(1, chips, add, total)
    for q in range(total_pieces):
        both = own_rows[:, q * piece : (q + 1) * piece]
        stream = jnp.where(core == 0, both[:out_rows], both[out_rows:])
        out_ref[:, q * piece : (q + 1) * piece] = (
            stream + mine_block[q * out_rows : (q + 1) * out_rows, :]
        ).astype(jnp.bfloat16)

    def drain(j, carry):
        scatter(j).wait_send()
        exchange((chip + j) % chips).wait_send()
        return carry

    lax.fori_loop(1, chips, drain, 0)
    exchange(chip).wait_send()
    gather_drain(attn_slots, attn_sems)
    gather_drain(gain_slots, gain_sems)
    gather_drain(stream_slots, stream_sems)


def rest_of_layer(shards, requests, drafts, attn, residual_in, norm_gain, *weights):
    rows, width = residual_in.shape
    out_proj, gate_w, up_w, down_w = weights
    depth = out_proj.shape[1]
    units = gate_w.shape[0]
    chips = shards // CORES
    out_rows = rows // shards
    piece = depth * out_rows // 16
    slots = (chips, 16, piece)
    bf16, f32 = jnp.bfloat16, jnp.float32
    vmem, hbm = pl.BlockSpec(memory_space=pltpu.VMEM), pl.BlockSpec(memory_space=pl.ANY)
    dma = pltpu.SemaphoreType.DMA
    return pl.pallas_call(
        functools.partial(layer_kernel, shards, requests, drafts),
        out_shape=jax.ShapeDtypeStruct((out_rows, depth), bf16),
        in_specs=[vmem] * 3 + [hbm] * 4,
        out_specs=vmem,
        scratch_shapes=[
            pltpu.VMEM(out_proj.shape, bf16),
            pltpu.VMEM(gate_w.shape, bf16),
            pltpu.VMEM(up_w.shape, bf16),
            pltpu.VMEM((2, units, piece), bf16),
            pltpu.VMEM((shards,) + attn.shape, bf16),
            pltpu.VMEM((shards, 1, width), f32),
            pltpu.VMEM((shards, rows, width), bf16),
            pltpu.VMEM((rows, depth), bf16),
            pltpu.VMEM((rows, depth), f32),
            pltpu.VMEM((CORES * out_rows, depth), f32),
            pltpu.VMEM((1, depth), f32),
            pltpu.VMEM((rows, units), bf16),
            pltpu.VMEM((16, piece), f32),
            pltpu.VMEM((16, piece), f32),
            pltpu.VMEM(slots, bf16),
            pltpu.VMEM(slots, bf16),
            pltpu.VMEM(slots, bf16),
            pltpu.VMEM(slots, bf16),
            dma((3 + depth // piece,)),
            dma((4, chips)),
            dma((4, chips)),
            dma((4, chips)),
            dma((2, chips)),
            dma((2, chips)),
        ],
        compiler_params=pltpu.CompilerParams(
            collective_id=0, has_side_effects=True, vmem_limit_bytes=60 * 1024 * 1024
        ),
        cost_estimate=pl.CostEstimate(
            flops=2 * rows * (depth * width + 3 * depth * units),
            bytes_accessed=2 * (depth * width + 3 * depth * units),
            transcendentals=rows * units,
        ),
    )(attn, residual_in, norm_gain.astype(f32).reshape(1, width), *weights)

def on_device(
    shards,
    residual_in,
    queries,
    key_cache,
    value_cache,
    new_keys,
    new_values,
    cache_len,
    tree_mask,
    out_proj,
    norm_gain,
    gate_w,
    up_w,
    down_w,
):
    blocks = queries.shape[0]
    drafts = queries.shape[1]
    requests = cache_len.shape[0]
    first_pair = lax.axis_index("shard") * blocks
    pair_index = first_pair + jnp.arange(blocks, dtype=jnp.int32)
    req_index = pair_index % requests
    req_pick = (req_index[:, None] == jnp.arange(requests, dtype=jnp.int32)[None, :]).astype(
        jnp.int32
    )
    lengths = jnp.sum(req_pick * cache_len[None, :], axis=1)
    tree_rows = jnp.einsum("br,rij->bij", req_pick, tree_mask)
    head_rows = queries.reshape(blocks, drafts, G, HD)
    score_scale = 1.0 / math.sqrt(HD)
    cache_scores = (
        jnp.einsum("bdgk,blk->bdgl", head_rows, key_cache, preferred_element_type=jnp.float32)
        * score_scale
    )
    draft_scores = (
        jnp.einsum("bdgk,bek->bdge", head_rows, new_keys, preferred_element_type=jnp.float32)
        * score_scale
    )
    valid_keys = jnp.arange(key_cache.shape[1], dtype=jnp.int32)[None, :] < lengths[:, None]
    cache_scores = jnp.where(valid_keys[:, None, None, :], cache_scores, -1e30)
    draft_scores = jnp.where(tree_rows[:, :, None, :] > 0, draft_scores, -1e30)
    peak_score = jnp.maximum(jnp.max(cache_scores, axis=-1), jnp.max(draft_scores, axis=-1))
    cache_weights = jnp.where(
        valid_keys[:, None, None, :], jnp.exp(cache_scores - peak_score[..., None]), 0.0
    )
    draft_weights = jnp.where(
        tree_rows[:, :, None, :] > 0, jnp.exp(draft_scores - peak_score[..., None]), 0.0
    )
    denom = jnp.sum(cache_weights, axis=-1) + jnp.sum(draft_weights, axis=-1)
    weighted = jnp.einsum(
        "bdgl,blk->bdgk",
        cache_weights.astype(jnp.bfloat16),
        value_cache,
        preferred_element_type=jnp.float32,
    )
    weighted = weighted + jnp.einsum(
        "bdge,bek->bdgk",
        draft_weights.astype(jnp.bfloat16),
        new_values,
        preferred_element_type=jnp.float32,
    )
    attn = (weighted / denom[..., None]).astype(jnp.bfloat16).reshape(blocks, drafts, G * HD)
    return rest_of_layer(
        shards,
        requests,
        drafts,
        attn.reshape(blocks * drafts, G * HD),
        residual_in,
        norm_gain,
        out_proj.T,
        gate_w.T,
        up_w.T,
        down_w,
    )


def solution(mesh):
    placed = (
        P("groups", "shard"),
        P(("groups", "shard"), None, None),
        P(("groups", "shard"), None, None),
        P(("groups", "shard"), None, None),
        P(("groups", "shard"), None, None),
        P(("groups", "shard"), None, None),
        P("groups"),
        P("groups", None, None),
        P(None, "shard"),
        P("shard"),
        P(None, "shard"),
        P(None, "shard"),
        P("shard", None),
    )
    return jax.shard_map(
        functools.partial(on_device, mesh.shape["shard"]),
        mesh=mesh,
        in_specs=placed,
        out_specs=P(("groups", "shard"), None),
        check_vma=False,
    )
```
